256 devices in a mesh: layer: 32 (over x, z), col: 8 (over y, core).
Axes of the slice: x: 4, y: 4, z: 8, core: 2. Of those that a mesh axis runs over, the one named last changes fastest.
Arguments:
- inputs: bfloat16 [4, 512, 5120], P(None, None, 'col'), may hold values from -6 to 6
- targets: bfloat16 [512, 4, 5120], P('layer', None, 'col'), may hold values from -6 to 6
- enc_weight: bfloat16 [4, 5120, 8192], P(None, 'col', 'layer'), may hold values from -0.078125 to 0.078125
- enc_bias: bfloat16 [4, 8192], P(None, 'layer'), may hold values from -3 to 3
- dec_weight: bfloat16 [10, 8192, 5120], P(None, 'layer', 'col'), may hold values from -0.0625 to 0.0625
- active_blocks: int32 [4, 4, 64], P(None, None, 'layer'), may hold values 0 or 1
Outputs:
- enc_grad: bfloat16 [4, 5120, 8192], P(None, 'col', 'layer')
- enc_bias_grad: float32 [4, 8192], P(None, 'layer')
- dec_grad: bfloat16 [10, 8192, 5120], P(None, 'layer', 'col')
The draws below stay inside these ranges and needn't reach their ends.
All inputs are finite; a program needn't handle non-finite values. No bound on the sum of `active_blocks` on one device may be relied on, other than what follows from the above.
Results may differ from the reference program's by a relative error of at most 0.023.
Values may be sent and summed in bfloat16 or wider, within the bound.
No kernel may reach another device: no remote copies, remote signals or barrier semaphores. Data moves between devices by JAX's collectives and lax.ppermute only.
A program may use at most 128 MiB of HBM per device.

```python
import jax
import jax.numpy as jnp

D = 5120
F = 8192
LAYERS = 4
TOKENS = 512
BLK = 128
PAIRS = 10
TBLK = 4
FBLK = 64


def set_ends(entries, stream_key, smallest, high):
    spot = [jax.random.randint(jax.random.fold_in(stream_key, axis), (), 0, length) for axis, length in enumerate(entries.shape)]
    longest = entries.shape.index(max(entries.shape))
    neighbour = spot[:longest] + [(spot[longest] + 1) % entries.shape[longest]] + spot[longest + 1:]
    return entries.at[tuple(spot)].set(smallest).at[tuple(neighbour)].set(high)


def shard_levels(own_key, shape, pieces, smallest, high):
    factor_of, own = 1.0, jax.random.fold_in(own_key, 6)
    for dim, parts in pieces:
        draws = jnp.exp(jax.random.uniform(jax.random.fold_in(own, dim), (parts,), jnp.float32, smallest / len(pieces), high / len(pieces)))
        factor_of = factor_of * jnp.repeat(draws, shape[dim] // parts).reshape([-1 if axis == dim else 1 for axis in range(len(shape))])
    return factor_of


def scatter_about(rng, extent, deviation, bound, shards=(), dtype=jnp.bfloat16):
    loudness = shard_levels(rng, extent, shards, -0.22, 0.18) if shards else 1.0
    array = jax.random.normal(rng, extent, jnp.float32) * deviation * loudness
    return jnp.minimum(jnp.maximum(array, -bound), bound).astype(dtype)


def setup_inputs(seed: int = 0) -> dict:
    keys = jax.random.split(jax.random.key(seed), 7)
    return {
        "inputs": scatter_about(keys[0], (LAYERS, TOKENS, D), 1.0, 6.0, ((2, 8),)),
        "targets": scatter_about(keys[1], (TOKENS, LAYERS, D), 1.0, 6.0, ((0, 32), (2, 8))),
        "enc_weight": scatter_about(keys[2], (LAYERS, D, F), D ** -0.5, 0.078125, ((1, 8), (2, 32))),
        "enc_bias": scatter_about(keys[3], (LAYERS, F), 0.5, 3.0, ((1, 32),)),
        "dec_weight": scatter_about(keys[4], (PAIRS, F, D), F ** -0.5, 0.0625, ((1, 32), (2, 8))),
        "active_blocks": set_ends((jax.random.randint(keys[5], (LAYERS, TBLK, FBLK), 0, 2) < 1).astype(jnp.int32), jax.random.fold_in(keys[5], 1), 0, 1),
    }


def pair_index(source, target, layer_count):
    return source * layer_count - source * (source - 1) // 2 + target - source


def block_mask(active, block_width):
    layer_count, token_blocks, feat_blocks = active.shape
    spread = active.astype(jnp.float32)[:, :, None, :, None]
    spread = jnp.broadcast_to(spread, (layer_count, token_blocks, block_width, feat_blocks, block_width))
    return spread.reshape(layer_count, token_blocks * block_width, feat_blocks * block_width)


def reference(inputs, targets, enc_weight, enc_bias, dec_weight, active_blocks):
    block_on = block_mask(active_blocks, BLK)
    features = []
    for source in range(LAYERS):
        preact = jnp.dot(inputs[source], enc_weight[source], preferred_element_type=jnp.float32)
        preact = preact + enc_bias[source].astype(jnp.float32)
        features.append((jax.nn.relu(preact) * block_on[source]).astype(jnp.bfloat16))
    rounded = []
    for target in range(LAYERS):
        rebuilt = jnp.zeros((TOKENS, D), jnp.float32)
        for source in range(target + 1):
            rebuilt = rebuilt + jnp.dot(features[source], dec_weight[pair_index(source, target, LAYERS)], preferred_element_type=jnp.float32)
        rounded.append((rebuilt - targets[:, target].astype(jnp.float32)).astype(jnp.bfloat16))
    dec_terms = []
    enc_terms = []
    bias_terms = []
    for source in range(LAYERS):
        feat_grad = jnp.zeros((TOKENS, F), jnp.float32)
        for target in range(source, LAYERS):
            pair = pair_index(source, target, LAYERS)
            dec_terms.append(jnp.dot(features[source].T, rounded[target], preferred_element_type=jnp.float32).astype(jnp.bfloat16))
            feat_grad = feat_grad + jnp.dot(rounded[target], dec_weight[pair].T, preferred_element_type=jnp.float32)
        pre_grad = jnp.where(features[source] > 0, feat_grad, jnp.zeros_like(feat_grad)).astype(jnp.bfloat16)
        enc_terms.append(jnp.dot(inputs[source].T, pre_grad, preferred_element_type=jnp.float32).astype(jnp.bfloat16))
        bias_terms.append(jnp.sum(pre_grad.astype(jnp.float32), axis=0))
    return jnp.stack(enc_terms), jnp.stack(bias_terms), jnp.stack(dec_terms)
```

```python
import jax
import jax.numpy as jnp
import numpy as np
from jax import lax
from jax.sharding import Mesh, PartitionSpec as P

F32, BF16 = jnp.float32, jnp.bfloat16
NX, NZ, NY, NC = 4, 8, 4, 2
ROWS = 16
LAYERS = 4
GROUPS = ((0, 1), (2, 3))


def pair(source, target):
    return source * LAYERS - source * (source - 1) // 2 + target - source


def shift(value, axis, size, by):
    return lax.ppermute(value, axis, [(i, (i + by) % size) for i in range(size)])


def target_moves():
    moves = []
    for x in range(NX):
        for z in range(NZ):
            for y in range(NY):
                for c in range(NC):
                    core, row = (c + z // NY) % NC, (y + z % NY) % NY
                    group = core * (NY * NX) + row * NX + x
                    source = ((group // NZ * NZ + group % NZ) * NY + y) * NC + c
                    dest = ((x * NZ + z) * NY + y) * NC + c
                    moves.append((source, dest))
    return moves


def own_order(inputs, x, y, c):
    layers, tokens, width = inputs.shape
    g = inputs.reshape(layers, NC, NY, NX, ROWS, width)
    order_c = (c + jnp.arange(NC)) % NC
    order_y = (y + jnp.arange(NY)) % NY
    order_x = (x + jnp.arange(NX)) % NX
    idx = (order_c[:, None, None] * NY + order_y[None, :, None]) * NX + order_x[None, None, :]
    g = inputs.reshape(layers, NC * NY * NX, ROWS, width)
    return jnp.take(g, idx.reshape(-1), axis=1).reshape(layers, tokens, width)


def dot(a, b, dims):
    return lax.dot_general(a, b, (dims, ((), ())), preferred_element_type=F32)


def gather_col(own):
    parts = [own] + [shift(own, "y", NY, -k) for k in range(1, NY)]
    mine = jnp.stack(parts, axis=1)
    other = shift(mine, "core", NC, 1)
    both = jnp.stack([mine, other], axis=1)
    return both.reshape(own.shape[0], -1, own.shape[2])


def scatter_col(keep, send, wire):
    other = shift(send, "core", NC, 1)
    half = keep.astype(F32) + other.astype(F32)
    g, rows, feats = half.shape
    half = half.reshape(g, NY, rows // NY, feats)
    total = half[:, 0]
    sent = half.astype(wire)
    for k in range(1, NY):
        total = total + shift(sent[:, k], "y", NY, k).astype(F32)
    return total


def body(inputs, targets, enc_weight, enc_bias, dec_weight, active_blocks):
    x, z, y, c = (lax.axis_index(a) for a in ("x", "z", "y", "core"))
    width = inputs.shape[2]
    feats = enc_weight.shape[2]
    tokens = inputs.shape[1]
    half = tokens // 2
    own_targets = lax.ppermute(targets, ("x", "z", "y", "core"), target_moves())
    own_targets = own_targets.transpose(1, 0, 2).astype(F32)
    ordered = own_order(inputs, x, y, c)
    own_active = lax.dynamic_index_in_dim(active_blocks, c * 2 + y // 2, axis=1, keepdims=False)
    own_mask = jnp.repeat(own_active.astype(F32), feats // own_active.shape[1], axis=1)[:, None, :]
    features, own_feats = [None] * LAYERS, [None] * LAYERS
    resid = []
    for group in GROUPS:
        lo, hi = group[0], group[-1] + 1
        part = jnp.einsum("ltd,ldf->ltf", ordered[lo:hi], enc_weight[lo:hi], preferred_element_type=F32)
        pre = scatter_col(part[:, :half], part[:, half:], F32) + enc_bias[lo:hi].astype(F32)[:, None, :]
        own = (jax.nn.relu(pre) * own_mask[lo:hi]).astype(BF16)
        whole = gather_col(own)
        for l in group:
            own_feats[l], features[l] = own[l - lo], whole[l - lo]
        terms = []
        for target in group:
            acc = dot(features[0], dec_weight[pair(0, target)], ((1,), (0,)))
            for source in range(1, target + 1):
                acc = acc + dot(features[source], dec_weight[pair(source, target)], ((1,), (0,)))
            terms.append(acc.astype(BF16).reshape(NZ, NX, ROWS, width))
        terms = jnp.stack(terms)
        total = terms[:, :, 0].astype(F32)
        for k in range(1, NX):
            total = total + shift(terms[:, :, k], "x", NX, k).astype(F32)
        total = total.astype(BF16)
        twice = jnp.concatenate([total, total], axis=1)
        rolled = lax.dynamic_slice_in_dim(twice, z, NZ, axis=1)
        acc = rolled[:, 0].astype(F32)
        for k in range(1, NZ):
            acc = acc + shift(rolled[:, k], "z", NZ, k).astype(F32)
        mine = (acc - own_targets[lo:hi]).astype(BF16)
        parts = jnp.stack([mine] + [shift(mine, "z", NZ, -k) for k in range(1, NZ)], axis=1)
        twice = jnp.concatenate([parts, parts], axis=1)
        line = lax.dynamic_slice_in_dim(twice, (NZ - z) % NZ, NZ, axis=1)
        plane = jnp.stack([line] + [shift(line, "x", NX, -k) for k in range(1, NX)], axis=2)
        plane = plane.reshape(len(group), tokens, width)
        resid += [plane[i] for i in range(len(group))]
    keeps, sends = [], []
    for source in range(LAYERS):
        acc = dot(resid[source], dec_weight[pair(source, source)], ((1,), (1,)))
        for target in range(source + 1, LAYERS):
            acc = acc + dot(resid[target], dec_weight[pair(source, target)], ((1,), (1,)))
        keeps.append(acc[:half])
        sends.append(acc[half:].astype(BF16))
    dec_grad = jnp.stack(
        [dot(features[s], resid[t], ((0,), (0,))).astype(BF16) for s in range(LAYERS) for t in range(s, LAYERS)]
    )
    fg = scatter_col(jnp.stack(keeps), jnp.stack(sends), BF16)
    own_grad = jnp.where(jnp.stack(own_feats) > 0, fg, 0.0).astype(BF16)
    pre_grad = gather_col(own_grad)
    enc_grad = jnp.einsum("ltd,ltf->ldf", ordered, pre_grad, preferred_element_type=F32).astype(BF16)
    bias_grad = jnp.sum(pre_grad.astype(F32), axis=1)
    return enc_grad, bias_grad, dec_grad


def solution(mesh):
    grid = Mesh(mesh.devices.reshape(NX, NZ, NY, NC), ("x", "z", "y", "core"))
    lay, col = ("x", "z"), ("y", "core")
    return jax.shard_map(
        body,
        mesh=grid,
        in_specs=(P(None, None, col), P(lay, None, col), P(None, col, lay), P(None, lay), P(None, lay, col), P(None, None, lay)),
        out_specs=(P(None, col, lay), P(None, lay), P(None, lay, col)),
        check_vma=False,
    )
```

```python
import functools

import jax
import jax.numpy as jnp
from jax import lax
from jax.experimental import pallas as pl
from jax.experimental.pallas import tpu as pltpu
from jax.sharding import Mesh, PartitionSpec as P

F32, BF16 = jnp.float32, jnp.bfloat16
NX, NZ, NY, NC = 4, 8, 4, 2
ROWS = 16
LAYERS = 4
OWN = ROWS * NX
HALF = LAYERS // 2
VMEM = pl.BlockSpec(memory_space=pltpu.VMEM)
SMEM = pl.BlockSpec(memory_space=pltpu.SMEM)


def pair(source, target):
    return source * LAYERS - source * (source - 1) // 2 + target - source


def shift(value, axis, size, by):
    return lax.ppermute(value, axis, [(i, (i + by) % size) for i in range(size)])


def target_moves():
    moves = []
    for x in range(NX):
        for z in range(NZ):
            for y in range(NY):
                for c in range(NC):
                    core, row = (c + z // NY) % NC, (y + z % NY) % NY
                    group = core * (NY * NX) + row * NX + x
                    moves.append(((group * NY + y) * NC + c, ((x * NZ + z) * NY + y) * NC + c))
    return moves


def spots():
    x, y, c = lax.axis_index("x"), lax.axis_index("y"), lax.axis_index("core")
    out = []
    for a in range(NC):
        for b in range(NY):
            for q in range(NX):
                group = (lax.rem(c + a, NC) * NY + lax.rem(y + b, NY)) * NX + lax.rem(x + q, NX)
                out.append(pl.multiple_of(group * ROWS, ROWS))
    return out


def call(kernel, outs, ins, name, grid=None, in_specs=None, out_specs=None, scratch=(), flops=0):
    moved = sum(i.size * i.dtype.itemsize for i in ins) + sum(
        functools.reduce(lambda u, v: u * v, o.shape) * o.dtype.itemsize for o in outs
    )
    extra = {} if grid is None else {"grid": grid}
    return pl.pallas_call(
        kernel,
        out_shape=tuple(outs),
        in_specs=in_specs or [VMEM] * len(ins),
        out_specs=tuple(out_specs or [VMEM] * len(outs)),
        scratch_shapes=list(scratch),
        compiler_params=pltpu.CompilerParams(vmem_limit_bytes=28 * 2**20),
        cost_estimate=pl.CostEstimate(flops=flops, bytes_accessed=moved, transcendentals=0),
        name=name,
        **extra,
    )(*ins)


def shape(dims, dtype):
    return jax.ShapeDtypeStruct(dims, dtype)


def per_layer(*dims):
    return pl.BlockSpec((1,) + dims, lambda l: (l,) + (0,) * len(dims))


def encode(inputs, enc_weight):
    layers, tokens, width = inputs.shape
    feats = enc_weight.shape[2]
    half = tokens // NC

    def kernel(in_ref, w_ref, keep_ref, send_ref, xs):
        for place, row in enumerate(spots()):
            xs[pl.ds(place * ROWS, ROWS), :] = in_ref[0, pl.ds(row, ROWS), :]
        send_ref[0] = jnp.dot(xs[half:], w_ref[0], preferred_element_type=F32)
        keep_ref[0] = jnp.dot(xs[:half], w_ref[0], preferred_element_type=F32)

    piece = shape((layers, half, feats), F32)
    return call(
        kernel, [piece, piece], [inputs, enc_weight], "encode", (layers,),
        [per_layer(tokens, width), per_layer(width, feats)], [per_layer(half, feats)] * 2,
        [pltpu.VMEM((tokens, width), BF16)], 2 * layers * tokens * width * feats,
    )


def split_half(keep, other, wire):
    layers, half, feats = keep.shape

    def kernel(keep_ref, other_ref, *outs):
        total = keep_ref[0].astype(F32) + other_ref[0].astype(F32)
        for b in range(NY):
            outs[b][0] = total[b * OWN : (b + 1) * OWN].astype(outs[b].dtype)

    outs = [shape((layers, OWN, feats), F32 if b == 0 else wire) for b in range(NY)]
    return call(
        kernel, outs, [keep, other], "half_sum", (layers,), [per_layer(half, feats)] * 2, [per_layer(OWN, feats)] * NY
    )


def activate(parts, bias, active):
    layers, own, feats = parts[0].shape
    blocks = active.shape[2]
    wide = feats // blocks

    def kernel(*refs):
        *part_refs, bias_ref, active_ref, out_ref = refs
        block = lax.axis_index("core") * 2 + lax.axis_index("y") // 2
        for l in range(layers):
            pre = part_refs[0][l]
            for ref in part_refs[1:]:
                pre = pre + ref[l]
            pre = jnp.maximum(pre + bias_ref[l : l + 1, :].astype(F32), 0.0)
            for j in range(blocks):
                on = active_ref[l, block, j].astype(F32)
                out_ref[l, :, j * wide : (j + 1) * wide] = (pre[:, j * wide : (j + 1) * wide] * on).astype(BF16)

    ins = [*parts, bias, active]
    return call(
        kernel, [shape((layers, own, feats), BF16)], ins, "activate", in_specs=[VMEM] * (len(ins) - 1) + [SMEM]
    )[0]


def decode(parts, dec_weight):
    layers, own, feats = parts[0].shape
    pairs, _, width = dec_weight.shape
    tokens = own * len(parts)

    def source_target(i):
        t = (i >= 1) * 1 + (i >= 3) * 1 + (i >= 6) * 1
        return i - t * (t + 1) // 2, t

    def kernel(*refs):
        part_refs, w_ref = refs[: len(parts)], refs[len(parts)]
        out_refs, feat_ref, acc = refs[len(parts) + 1 : len(parts) + 1 + 2 * NX], refs[-2], refs[-1]
        i = pl.program_id(0)
        source, target = source_target(i)

        @pl.when(i == 0)
        def _():
            for l in range(layers):
                for k, ref in enumerate(part_refs):
                    feat_ref[l, pl.ds(k * own, own), :] = ref[l]

        term = jnp.dot(feat_ref[source], w_ref[0], preferred_element_type=F32)

        @pl.when(source == 0)
        def _():
            acc[...] = term

        @pl.when(source > 0)
        def _():
            acc[...] += term

        for h in range(2):

            @pl.when((source == target) & (target // HALF == h))
            def _():
                for s in range(NZ):
                    for q in range(NX):
                        out_refs[h * NX + q][0, s] = acc[pl.ds((s * NX + q) * ROWS, ROWS), :].astype(BF16)

    def weight_at(i):
        s, t = source_target(i)
        return (s * LAYERS - s * (s - 1) // 2 + t - s, 0, 0)

    def half_spec(h):
        return pl.BlockSpec((1, NZ, ROWS, width), lambda i: (jnp.clip(source_target(i)[1] - h * HALF, 0, HALF - 1), 0, 0, 0))

    outs = [shape((HALF, NZ, ROWS, width), BF16)] * (2 * NX) + [shape((layers, tokens, feats), BF16)]
    out_specs = [half_spec(0)] * NX + [half_spec(1)] * NX + [VMEM]
    *terms, features = call(
        kernel, outs, [*parts, dec_weight], "decode", (pairs,),
        [VMEM] * len(parts) + [pl.BlockSpec((1, feats, width), weight_at)], out_specs,
        [pltpu.VMEM((tokens, width), F32)], 2 * pairs * tokens * feats * width,
    )
    return terms[:NX], terms[NX:], features


def relay(ours, passing):
    block = (1,) + ours[0].shape[1:]

    def kernel(*refs):
        for k in range(2):
            refs[4 + k][...] = (refs[k][...].astype(F32) + refs[2 + k][...].astype(F32)).astype(BF16)

    spec = pl.BlockSpec(block, lambda l: (l, 0, 0, 0))
    return call(
        kernel, [shape(ours[0].shape, BF16)] * 2, [*ours, *passing], "relay", (ours[0].shape[0],), [spec] * 4, [spec] * 2
    )


def line_sum(low, high):
    targets, _, rows, width = low[0].shape
    count = len(low)

    def kernel(*refs):
        z = lax.axis_index("z")
        out_refs = refs[2 * count :]
        for h in range(2):
            part_refs = refs[h * count : (h + 1) * count]
            for j in range(NZ):
                s = lax.rem(z + j, NZ)
                for l in range(targets):
                    total = part_refs[0][l, s].astype(F32)
                    for ref in part_refs[1:]:
                        total = total + ref[l, s].astype(F32)
                    out_refs[j][h * targets + l] = total.astype(BF16)

    return call(kernel, [shape((2 * targets, rows, width), BF16)] * NZ, [*low, *high], "line_sum")


def residual_rows(parts, own_targets):
    layers, rows, width = parts[0].shape

    def kernel(*refs):
        part_refs, target_ref, out_ref = refs[:NZ], refs[NZ], refs[NZ + 1]
        for l in range(layers):
            total = part_refs[0][l].astype(F32)
            for ref in part_refs[1:]:
                total = total + ref[l].astype(F32)
            out_ref[l] = (total - target_ref[l].astype(F32)).astype(BF16)

    return call(kernel, [shape((layers, rows, width), BF16)], [*parts, own_targets], "residual")[0]


def line_up(parts):
    layers, rows, width = parts[0].shape

    def kernel(*refs):
        part_refs, out_refs = refs[:NZ], refs[NZ:]
        z = lax.axis_index("z")
        for j in range(NZ):
            s = lax.rem(z + j, NZ)
            for l in range(layers):
                out_refs[l // HALF][l % HALF, s] = part_refs[j][l]

    return call(kernel, [shape((HALF, NZ, rows, width), BF16)] * 2, parts, "line_up")


def assemble(refs, out):
    for l in range(out.shape[0]):
        for s in range(NZ):
            for q in range(NX):
                out[l, pl.ds((s * NX + q) * ROWS, ROWS), :] = refs[l // HALF * NX + q][l % HALF, s]


def backward(planes, dec_weight):
    pairs, feats, width = dec_weight.shape
    layers = LAYERS
    tokens = NZ * NX * ROWS
    half = tokens // NC

    def source_target(i):
        s = (i >= 4) * 1 + (i >= 7) * 1 + (i >= 9) * 1
        return s, i - (s * LAYERS - s * (s - 1) // 2) + s

    def kernel(*refs):
        plane_refs, (w_ref, keep_ref, send_ref, resid, acc) = refs[: len(planes)], refs[len(planes) :]
        i = pl.program_id(0)
        source, target = source_target(i)

        @pl.when(i == 0)
        def _():
            assemble(plane_refs, resid)

        term = lax.dot_general(resid[target], w_ref[0], (((1,), (1,)), ((), ())), preferred_element_type=F32)

        @pl.when(source == target)
        def _():
            acc[...] = term

        @pl.when(source != target)
        def _():
            acc[...] += term

        @pl.when(target == layers - 1)
        def _():
            keep_ref[0] = acc[pl.ds(0, half), :]
            send_ref[0] = acc[pl.ds(half, half), :].astype(BF16)

    where = pl.BlockSpec((1, half, feats), lambda i: (source_target(i)[0], 0, 0))
    return call(
        kernel, [shape((layers, half, feats), F32), shape((layers, half, feats), BF16)], [*planes, dec_weight],
        "backward", (pairs,), [VMEM] * len(planes) + [pl.BlockSpec((1, feats, width), lambda i: (i, 0, 0))], [where, where],
        [pltpu.VMEM((layers, tokens, width), BF16), pltpu.VMEM((tokens, feats), F32)],
        2 * pairs * tokens * feats * width,
    )


def decoder_grads(features, planes):
    layers, tokens, feats = features.shape
    width = planes[0].shape[3]
    pairs = layers * (layers + 1) // 2

    def source_target(i):
        s = (i >= 4) * 1 + (i >= 7) * 1 + (i >= 9) * 1
        return s, i - (s * LAYERS - s * (s - 1) // 2) + s

    def kernel(*refs):
        plane_refs, (feat_ref, out_ref, resid) = refs[: len(planes)], refs[len(planes) :]
        i = pl.program_id(0)
        source, target = source_target(i)

        @pl.when(i == 0)
        def _():
            assemble(plane_refs, resid)

        out_ref[0] = lax.dot_general(
            feat_ref[source], resid[target], (((0,), (0,)), ((), ())), preferred_element_type=F32
        ).astype(BF16)

    return call(
        kernel, [shape((pairs, feats, width), BF16)], [*planes, features], "decoder_grads", (pairs,),
        [VMEM] * (len(planes) + 1), [pl.BlockSpec((1, feats, width), lambda i: (i, 0, 0))],
        [pltpu.VMEM((layers, tokens, width), BF16)], 2 * pairs * tokens * feats * width,
    )[0]


def mask_grad(parts, own_feats):
    layers, own, feats = own_feats.shape

    def kernel(*refs):
        part_refs, feat_ref, out_ref = refs[:NY], refs[NY], refs[NY + 1]
        for l in range(layers):
            total = part_refs[0][l].astype(F32)
            for ref in part_refs[1:]:
                total = total + ref[l].astype(F32)
            out_ref[l] = jnp.where(feat_ref[l].astype(F32) > 0, total, 0.0).astype(BF16)

    return call(kernel, [shape((layers, own, feats), BF16)], [*parts, own_feats], "mask_grad")[0]


def encoder_grads(parts, inputs):
    layers, tokens, width = inputs.shape
    own, feats = parts[0].shape[1:]

    def kernel(*refs):
        part_refs, (in_ref, grad_ref, bias_ref, whole) = refs[: len(parts)], refs[len(parts) :]
        total = jnp.zeros((1, feats), F32)
        places = spots()
        for k, ref in enumerate(part_refs):
            for q in range(NX):
                whole[pl.ds(places[k * NX + q], ROWS), :] = ref[0, q * ROWS : (q + 1) * ROWS, :]
            total = total + jnp.sum(ref[0].astype(F32), axis=0, keepdims=True)
        bias_ref[0] = total
        grad_ref[0] = lax.dot_general(
            in_ref[0], whole[...], (((0,), (0,)), ((), ())), preferred_element_type=F32
        ).astype(BF16)

    grad, bias = call(
        kernel, [shape((layers, width, feats), BF16), shape((layers, 1, feats), F32)], [*parts, inputs],
        "encoder_grads", (layers,), [per_layer(own, feats)] * len(parts) + [per_layer(tokens, width)],
        [per_layer(width, feats), per_layer(1, feats)], [pltpu.VMEM((tokens, feats), BF16)],
        2 * layers * tokens * width * feats,
    )
    return grad, bias.reshape(layers, feats)


def gather_col(own):
    mine = [own] + [shift(own, "y", NY, -k) for k in range(1, NY)]
    return mine + [shift(part, "core", NC, 1) for part in mine]


def scatter_col(pieces):
    return [pieces[0]] + [shift(pieces[k], "y", NY, k) for k in range(1, NY)]


def scatter_x(low, high):
    passing = [shift(low[2], "x", NX, 1), shift(high[2], "x", NX, -1)]
    high_1, low_3 = shift(high[1], "x", NX, 1), shift(low[3], "x", NX, -1)
    low_1, high_3 = relay([low[1], high[3]], passing)
    low_1, high_3 = shift(low_1, "x", NX, 1), shift(high_3, "x", NX, -1)
    return [low[0], low_1, low_3], [high[0], high_1, high_3]


def gather_x(low, high):
    low_3, high_1 = shift(low, "x", NX, 1), shift(high, "x", NX, -1)
    high_3, low_1 = shift(high, "x", NX, 1), shift(low, "x", NX, -1)
    low_2, high_2 = shift(low_3, "x", NX, 1), shift(high_1, "x", NX, -1)
    return [low, low_1, low_2, low_3, high, high_1, high_2, high_3]


def body(inputs, targets, enc_weight, enc_bias, dec_weight, active_blocks):
    keep, send = encode(inputs, enc_weight)
    keep, targets = lax.optimization_barrier((keep, targets))
    own_targets = lax.ppermute(targets, ("x", "z", "y", "core"), target_moves()).transpose(1, 0, 2)
    pieces = split_half(keep, shift(send, "core", NC, 1), F32)
    own_feats = activate(scatter_col(pieces), enc_bias, active_blocks)
    low, high, features = decode(gather_col(own_feats), dec_weight)
    pieces = line_sum(*scatter_x(low, high))
    mine = residual_rows([pieces[0]] + [shift(pieces[k], "z", NZ, k) for k in range(1, NZ)], own_targets)
    low, high = line_up([mine] + [shift(mine, "z", NZ, -k) for k in range(1, NZ)])
    planes = gather_x(low, high)
    keep, send = backward(planes, dec_weight)
    pieces = split_half(keep, shift(send, "core", NC, 1), BF16)
    pieces, features = lax.optimization_barrier((pieces, features))
    dec_grad = decoder_grads(features, planes)
    parts = scatter_col(pieces)
    parts, dec_grad = lax.optimization_barrier((parts, dec_grad))
    own_grad = mask_grad(parts, own_feats)
    enc_grad, bias_grad = encoder_grads(gather_col(own_grad), inputs)
    return enc_grad, bias_grad, dec_grad


def solution(mesh):
    grid = Mesh(mesh.devices.reshape(NX, NZ, NY, NC), ("x", "z", "y", "core"))
    lay, col = ("x", "z"), ("y", "core")
    return jax.shard_map(
        body,
        mesh=grid,
        in_specs=(P(None, None, col), P(lay, None, col), P(None, col, lay), P(None, lay), P(None, lay, col), P(None, None, lay)),
        out_specs=(P(None, col, lay), P(None, lay), P(None, lay, col)),
        check_vma=False,
    )
```

```python
import functools

import jax
import jax.numpy as jnp
from jax import lax
from jax.experimental import pallas as pl
from jax.experimental.pallas import tpu as pltpu
from jax.sharding import Mesh, PartitionSpec as P

F32, BF16 = jnp.float32, jnp.bfloat16
NX, NZ, NY, NC = 4, 8, 4, 2
ROWS = 16
LAYERS = 4
OWN = ROWS * NX
HALF = LAYERS // 2
Z_ORDER = (7, 1, 6, 2, 5, 3, 4)
VMEM = pl.BlockSpec(memory_space=pltpu.VMEM)
SMEM = pl.BlockSpec(memory_space=pltpu.SMEM)


def pair(source, target):
    return source * LAYERS - source * (source - 1) // 2 + target - source


def shift(value, axis, size, by):
    return lax.ppermute(value, axis, [(i, (i + by) % size) for i in range(size)])


def target_moves():
    moves = []
    for x in range(NX):
        for z in range(NZ):
            for y in range(NY):
                for c in range(NC):
                    core, row = (c + z // NY) % NC, (y + z % NY) % NY
                    group = core * (NY * NX) + row * NX + x
                    moves.append(((group * NY + y) * NC + c, ((x * NZ + z) * NY + y) * NC + c))
    return moves


def spots():
    x, y, c = lax.axis_index("x"), lax.axis_index("y"), lax.axis_index("core")
    out = []
    for a in range(NC):
        for b in range(NY):
            for q in range(NX):
                group = (lax.rem(c + a, NC) * NY + lax.rem(y + b, NY)) * NX + lax.rem(x + q, NX)
                out.append(pl.multiple_of(group * ROWS, ROWS))
    return out


def call(kernel, outs, ins, name, grid=None, in_specs=None, out_specs=None, scratch=(), flops=0, vmem=8):
    moved = sum(i.size * i.dtype.itemsize for i in ins) + sum(
        functools.reduce(lambda u, v: u * v, o.shape) * o.dtype.itemsize for o in outs
    )
    extra = {} if grid is None else {"grid": grid}
    return pl.pallas_call(
        kernel,
        out_shape=tuple(outs),
        in_specs=in_specs or [VMEM] * len(ins),
        out_specs=tuple(out_specs or [VMEM] * len(outs)),
        scratch_shapes=list(scratch),
        compiler_params=pltpu.CompilerParams(vmem_limit_bytes=vmem * 2**20),
        cost_estimate=pl.CostEstimate(flops=flops, bytes_accessed=moved, transcendentals=0),
        name=name,
        **extra,
    )(*ins)


def shape(dims, dtype):
    return jax.ShapeDtypeStruct(dims, dtype)


def per_layer(*dims):
    return pl.BlockSpec((1,) + dims, lambda l: (l,) + (0,) * len(dims))


def encode(inputs, enc_weight):
    layers, tokens, width = inputs.shape
    feats = enc_weight.shape[2]
    half = tokens // NC

    def kernel(in_ref, w_ref, keep_ref, send_ref, xs):
        for place, row in enumerate(spots()):
            xs[pl.ds(place * ROWS, ROWS), :] = in_ref[0, pl.ds(row, ROWS), :]
        send_ref[0] = jnp.dot(xs[half:], w_ref[0], preferred_element_type=F32)
        keep_ref[0] = jnp.dot(xs[:half], w_ref[0], preferred_element_type=F32)

    piece = shape((layers, half, feats), F32)
    return call(
        kernel, [piece, piece], [inputs, enc_weight], "encode", (layers,),
        [per_layer(tokens, width), per_layer(width, feats)], [per_layer(half, feats)] * 2,
        [pltpu.VMEM((tokens, width), BF16)], 2 * layers * tokens * width * feats, 12,
    )


def split_half(keep, other, wire):
    layers, half, feats = keep.shape

    def kernel(keep_ref, other_ref, *outs):
        total = keep_ref[0].astype(F32) + other_ref[0].astype(F32)
        for b in range(NY):
            outs[b][0] = total[b * OWN : (b + 1) * OWN].astype(outs[b].dtype)

    outs = [shape((layers, OWN, feats), F32 if b == 0 else wire) for b in range(NY)]
    return call(
        kernel, outs, [keep, other], "half_sum", (layers,), [per_layer(half, feats)] * 2, [per_layer(OWN, feats)] * NY
    )


def activate(parts, bias, active):
    layers, own, feats = parts[0].shape
    blocks = active.shape[2]
    wide = feats // blocks

    def kernel(*refs):
        *part_refs, bias_ref, active_ref, out_ref = refs
        block = lax.axis_index("core") * 2 + lax.axis_index("y") // 2
        for l in range(layers):
            pre = part_refs[0][l]
            for ref in part_refs[1:]:
                pre = pre + ref[l]
            pre = jnp.maximum(pre + bias_ref[l : l + 1, :].astype(F32), 0.0)
            for j in range(blocks):
                on = active_ref[l, block, j].astype(F32)
                out_ref[l, :, j * wide : (j + 1) * wide] = (pre[:, j * wide : (j + 1) * wide] * on).astype(BF16)

    ins = [*parts, bias, active]
    return call(
        kernel, [shape((layers, own, feats), BF16)], ins, "activate", in_specs=[VMEM] * (len(ins) - 1) + [SMEM]
    )[0]


def pick(i, values):
    out = values[0]
    for k in range(1, len(values)):
        out = jnp.where(i == k, values[k], out)
    return out


def decode(parts, dec_weight):
    layers, own, feats = parts[0].shape
    width = dec_weight.shape[2]
    tokens = own * len(parts)

    def kernel(*refs):
        part_refs, refs = refs[: len(parts)], refs[len(parts) :]
        w_refs, refs = refs[:layers], refs[layers:]
        out_refs, (feat_ref, weights) = refs[: 2 * NX], refs[2 * NX :]

        @pl.when(pl.program_id(0) == 0)
        def _():
            for l in range(layers):
                for k, ref in enumerate(part_refs):
                    feat_ref[pl.ds(k * own, own), l * feats : (l + 1) * feats] = ref[l]

        for t in range(layers):
            depth = (t + 1) * feats

            @pl.when(pl.program_id(0) == t)
            def _():
                for s in range(t + 1):
                    weights[pl.ds(s * feats, feats), :] = w_refs[s][0]
                total = jnp.dot(feat_ref[:, :depth], weights[:depth, :], preferred_element_type=F32).astype(BF16)
                for s in range(NZ):
                    for q in range(NX):
                        at = (s * NX + q) * ROWS
                        out_refs[t // HALF * NX + q][t % HALF, s] = total[at : at + ROWS]

    def weight(s):
        pairs = [pair(min(s, t), t) for t in range(layers)]
        return pl.BlockSpec((1, feats, width), lambda i: (pick(i, pairs), 0, 0))

    outs = [shape((HALF, NZ, ROWS, width), BF16)] * (2 * NX) + [shape((tokens, layers * feats), BF16)]
    flops = layers * (layers + 1) * tokens * feats * width
    *terms, features = call(
        kernel, outs, [*parts, *[dec_weight] * layers], "decode", (layers,),
        [VMEM] * len(parts) + [weight(s) for s in range(layers)], None,
        [pltpu.VMEM((layers * feats, width), BF16)], flops, 24,
    )
    return terms[:NX], terms[NX:], features


def relay(ours, passing):
    block = (1,) + ours[0].shape[1:]

    def kernel(*refs):
        for k in range(2):
            refs[4 + k][...] = (refs[k][...].astype(F32) + refs[2 + k][...].astype(F32)).astype(BF16)

    spec = pl.BlockSpec(block, lambda l: (l, 0, 0, 0))
    return call(
        kernel, [shape(ours[0].shape, BF16)] * 2, [*ours, *passing], "relay", (ours[0].shape[0],), [spec] * 4, [spec] * 2
    )


def line_sum(low, high):
    targets, _, rows, width = low[0].shape
    count = len(low)

    def kernel(*refs):
        z = lax.axis_index("z")
        out_refs = refs[2 * count :]
        for h in range(2):
            part_refs = refs[h * count : (h + 1) * count]
            for j in range(NZ):
                s = lax.rem(z + j, NZ)
                for l in range(targets):
                    total = part_refs[0][l, s].astype(F32)
                    for ref in part_refs[1:]:
                        total = total + ref[l, s].astype(F32)
                    out_refs[j][h * targets + l] = total.astype(BF16)

    return call(kernel, [shape((2 * targets, rows, width), BF16)] * NZ, [*low, *high], "line_sum")


def residual_rows(parts, own_targets):
    layers, rows, width = parts[0].shape

    def kernel(*refs):
        part_refs, target_ref, out_ref = refs[:NZ], refs[NZ], refs[NZ + 1]
        for l in range(layers):
            total = part_refs[0][l].astype(F32)
            for ref in part_refs[1:]:
                total = total + ref[l].astype(F32)
            out_ref[l] = (total - target_ref[l].astype(F32)).astype(BF16)

    return call(kernel, [shape((layers, rows, width), BF16)], [*parts, own_targets], "residual")[0]


def line_up(parts, order):
    layers, rows, width = parts[0].shape

    def kernel(*refs):
        part_refs, out_refs = refs[:NZ], refs[NZ:]
        z = lax.axis_index("z")
        for ref, j in zip(part_refs, order):
            s = lax.rem(z + j, NZ)
            for l in range(layers):
                out_refs[l // HALF][l % HALF, s] = ref[l]

    return call(kernel, [shape((HALF, NZ, rows, width), BF16)] * 2, parts, "line_up")


def assemble(refs, out):
    for l in range(out.shape[0]):
        for s in range(NZ):
            for q in range(NX):
                out[l, pl.ds((s * NX + q) * ROWS, ROWS), :] = refs[l // HALF * NX + q][l % HALF, s]


def backward(planes, dec_weight):
    feats, width = dec_weight.shape[1:]
    tokens = NZ * NX * ROWS
    half = tokens // NC

    def kernel(*refs):
        plane_refs, refs = refs[: len(planes)], refs[len(planes) :]
        w_refs, (keep_ref, send_ref, resid, weights) = refs[:LAYERS], refs[LAYERS:]

        @pl.when(pl.program_id(0) == 0)
        def _():
            for m in range(LAYERS):
                for s in range(NZ):
                    for q in range(NX):
                        at = pl.ds((s * NX + q) * ROWS, ROWS)
                        resid[at, m * width : (m + 1) * width] = plane_refs[m // HALF * NX + q][m % HALF, s]

        for l in range(LAYERS):

            @pl.when(pl.program_id(0) == l)
            def _():
                for m in range(l, LAYERS):
                    weights[:, m * width : (m + 1) * width] = w_refs[m][0]
                total = lax.dot_general(
                    resid[:, l * width :], weights[:, l * width :], (((1,), (1,)), ((), ())), preferred_element_type=F32
                )
                keep_ref[l] = total[:half]
                send_ref[l] = total[half:].astype(BF16)

    def weight(m):
        pairs = [pair(min(l, m), m) for l in range(LAYERS)]
        return pl.BlockSpec((1, feats, width), lambda i: (pick(i, pairs), 0, 0))

    flops = LAYERS * (LAYERS + 1) * tokens * feats * width
    return call(
        kernel, [shape((LAYERS, half, feats), F32), shape((LAYERS, half, feats), BF16)],
        [*planes, *[dec_weight] * LAYERS], "backward", (LAYERS,),
        [VMEM] * len(planes) + [weight(m) for m in range(LAYERS)], None,
        [pltpu.VMEM((tokens, LAYERS * width), BF16), pltpu.VMEM((feats, LAYERS * width), BF16)], flops, 28,
    )


def decoder_grads(features, planes):
    layers, tokens = LAYERS, features.shape[0]
    feats, width = features.shape[1] // layers, planes[0].shape[3]
    pairs = layers * (layers + 1) // 2

    def source_target(i):
        s = (i >= 4) * 1 + (i >= 7) * 1 + (i >= 9) * 1
        return s, i - (s * LAYERS - s * (s - 1) // 2) + s

    def kernel(*refs):
        plane_refs, (feat_ref, out_ref, resid) = refs[: len(planes)], refs[len(planes) :]
        i = pl.program_id(0)
        source, target = source_target(i)

        @pl.when(i == 0)
        def _():
            assemble(plane_refs, resid)

        out_ref[0] = lax.dot_general(
            feat_ref[:, pl.ds(pl.multiple_of(source * feats, feats), feats)], resid[target],
            (((0,), (0,)), ((), ())), preferred_element_type=F32,
        ).astype(BF16)

    return call(
        kernel, [shape((pairs, feats, width), BF16)], [*planes, features], "decoder_grads", (pairs,),
        [VMEM] * (len(planes) + 1), [pl.BlockSpec((1, feats, width), lambda i: (i, 0, 0))],
        [pltpu.VMEM((layers, tokens, width), BF16)], 2 * pairs * tokens * feats * width, 24,
    )[0]


def mask_grad(parts, own_feats):
    layers, own, feats = own_feats.shape

    def kernel(*refs):
        part_refs, feat_ref, out_ref = refs[:NY], refs[NY], refs[NY + 1]
        for l in range(layers):
            total = part_refs[0][l].astype(F32)
            for ref in part_refs[1:]:
                total = total + ref[l].astype(F32)
            out_ref[l] = jnp.where(feat_ref[l].astype(F32) > 0, total, 0.0).astype(BF16)

    return call(kernel, [shape((layers, own, feats), BF16)], [*parts, own_feats], "mask_grad")[0]


def encoder_grads(parts, inputs):
    layers, tokens, width = inputs.shape
    own, feats = parts[0].shape[1:]

    def kernel(*refs):
        part_refs, (in_ref, grad_ref, bias_ref, whole) = refs[: len(parts)], refs[len(parts) :]
        total = jnp.zeros((1, feats), F32)
        places = spots()
        for k, ref in enumerate(part_refs):
            for q in range(NX):
                whole[pl.ds(places[k * NX + q], ROWS), :] = ref[0, q * ROWS : (q + 1) * ROWS, :]
            total = total + jnp.sum(ref[0].astype(F32), axis=0, keepdims=True)
        bias_ref[pl.ds(pl.program_id(0), 1), :] = total
        grad_ref[0] = lax.dot_general(
            in_ref[0], whole[...], (((0,), (0,)), ((), ())), preferred_element_type=F32
        ).astype(BF16)

    grad, bias = call(
        kernel, [shape((layers, width, feats), BF16), shape((layers, feats), F32)], [*parts, inputs],
        "encoder_grads", (layers,), [per_layer(own, feats)] * len(parts) + [per_layer(tokens, width)],
        [per_layer(width, feats), VMEM], [pltpu.VMEM((tokens, feats), BF16)],
        2 * layers * tokens * width * feats, 16,
    )
    return grad, bias


def gather_col(own):
    mine = [own] + [shift(own, "y", NY, -k) for k in range(1, NY)]
    return mine + [shift(part, "core", NC, 1) for part in mine]


def scatter_col(pieces):
    return [pieces[0]] + [shift(pieces[k], "y", NY, k) for k in range(1, NY)]


def scatter_x(low, high):
    passing = [shift(low[2], "x", NX, 1), shift(high[2], "x", NX, -1)]
    high_1, low_3 = shift(high[1], "x", NX, 1), shift(low[3], "x", NX, -1)
    low_1, high_3 = relay([low[1], high[3]], passing)
    low_1, high_3 = shift(low_1, "x", NX, 1), shift(high_3, "x", NX, -1)
    return [low[0], low_1, low_3], [high[0], high_1, high_3]


def gather_x(low, high):
    low_3, high_1 = shift(low, "x", NX, 1), shift(high, "x", NX, -1)
    high_3, low_1 = shift(high, "x", NX, 1), shift(low, "x", NX, -1)
    low_2, high_2 = shift(low_3, "x", NX, 1), shift(high_1, "x", NX, -1)
    return [low, low_1, low_2, low_3, high, high_1, high_2, high_3]


def body(inputs, targets, enc_weight, enc_bias, dec_weight, active_blocks):
    keep, send = encode(inputs, enc_weight)
    keep, targets = lax.optimization_barrier((keep, targets))
    own_targets = lax.ppermute(targets, ("x", "z", "y", "core"), target_moves()).transpose(1, 0, 2)
    pieces = split_half(keep, shift(send, "core", NC, 1), F32)
    own_feats = activate(scatter_col(pieces), enc_bias, active_blocks)
    low, high, features = decode(gather_col(own_feats), dec_weight)
    pieces = line_sum(*scatter_x(low, high))
    mine = residual_rows([pieces[0]] + [shift(pieces[k], "z", NZ, k) for k in Z_ORDER], own_targets)
    low, high = line_up([mine] + [shift(mine, "z", NZ, -k) for k in Z_ORDER], (0,) + Z_ORDER)
    planes = gather_x(low, high)
    keep, send = backward(planes, dec_weight)
    pieces = split_half(keep, shift(send, "core", NC, 1), BF16)
    pieces, features = lax.optimization_barrier((pieces, features))
    dec_grad = decoder_grads(features, planes)
    parts = scatter_col(pieces)
    parts, dec_grad = lax.optimization_barrier((parts, dec_grad))
    own_grad = mask_grad(parts, own_feats)
    enc_grad, bias_grad = encoder_grads(gather_col(own_grad), inputs)
    return enc_grad, bias_grad, dec_grad


def solution(mesh):
    grid = Mesh(mesh.devices.reshape(NX, NZ, NY, NC), ("x", "z", "y", "core"))
    lay, col = ("x", "z"), ("y", "core")
    return jax.shard_map(
        body,
        mesh=grid,
        in_specs=(P(None, None, col), P(lay, None, col), P(None, col, lay), P(None, lay), P(None, lay, col), P(None, None, lay)),
        out_specs=(P(None, col, lay), P(None, lay), P(None, lay, col)),
        check_vma=False,
    )
```

```python
import functools

import jax
import jax.numpy as jnp
from jax import lax
from jax.experimental import pallas as pl
from jax.experimental.pallas import tpu as pltpu
from jax.sharding import Mesh, PartitionSpec as P

F32, BF16 = jnp.float32, jnp.bfloat16
NX, NZ, NY, NC = 4, 8, 4, 2
ROWS = 16
LAYERS = 4
OWN = ROWS * NX
HALF = LAYERS // 2
Z_ORDER = (7, 1, 6, 2, 5, 3, 4)
VMEM = pl.BlockSpec(memory_space=pltpu.VMEM)
SMEM = pl.BlockSpec(memory_space=pltpu.SMEM)


def pair(source, target):
    return source * LAYERS - source * (source - 1) // 2 + target - source


def shift(value, axis, size, by):
    return lax.ppermute(value, axis, [(i, (i + by) % size) for i in range(size)])


def target_moves():
    moves = []
    for x in range(NX):
        for z in range(NZ):
            for y in range(NY):
                for c in range(NC):
                    core, row = (c + z // NY) % NC, (y + z % NY) % NY
                    group = core * (NY * NX) + row * NX + x
                    moves.append(((group * NY + y) * NC + c, ((x * NZ + z) * NY + y) * NC + c))
    return moves


def spots():
    x, y, c = lax.axis_index("x"), lax.axis_index("y"), lax.axis_index("core")
    out = []
    for a in range(NC):
        for b in range(NY):
            for q in range(NX):
                group = (lax.rem(c + a, NC) * NY + lax.rem(y + b, NY)) * NX + lax.rem(x + q, NX)
                out.append(pl.multiple_of(group * ROWS, ROWS))
    return out


def call(kernel, outs, ins, name, grid=None, in_specs=None, out_specs=None, scratch=(), flops=0, vmem=8):
    moved = sum(i.size * i.dtype.itemsize for i in ins) + sum(
        functools.reduce(lambda u, v: u * v, o.shape) * o.dtype.itemsize for o in outs
    )
    extra = {} if grid is None else {"grid": grid}
    return pl.pallas_call(
        kernel,
        out_shape=tuple(outs),
        in_specs=in_specs or [VMEM] * len(ins),
        out_specs=tuple(out_specs or [VMEM] * len(outs)),
        scratch_shapes=list(scratch),
        compiler_params=pltpu.CompilerParams(vmem_limit_bytes=vmem * 2**20),
        cost_estimate=pl.CostEstimate(flops=flops, bytes_accessed=moved, transcendentals=0),
        name=name,
        **extra,
    )(*ins)


def shape(dims, dtype):
    return jax.ShapeDtypeStruct(dims, dtype)


def per_layer(*dims):
    return pl.BlockSpec((1,) + dims, lambda l: (l,) + (0,) * len(dims))


def encode(inputs, enc_weight):
    layers, tokens, width = inputs.shape
    feats = enc_weight.shape[2]
    half = tokens // NC

    def kernel(in_ref, w_ref, keep_ref, send_ref, xs):
        for place, row in enumerate(spots()):
            xs[pl.ds(place * ROWS, ROWS), :] = in_ref[0, pl.ds(row, ROWS), :]
        send_ref[0] = jnp.dot(xs[half:], w_ref[0], preferred_element_type=F32)
        keep_ref[0] = jnp.dot(xs[:half], w_ref[0], preferred_element_type=F32)

    piece = shape((layers, half, feats), F32)
    return call(
        kernel, [piece, piece], [inputs, enc_weight], "encode", (layers,),
        [per_layer(tokens, width), per_layer(width, feats)], [per_layer(half, feats)] * 2,
        [pltpu.VMEM((tokens, width), BF16)], 2 * layers * tokens * width * feats, 12,
    )


def split_half(keep, other, wire):
    layers, half, feats = keep.shape

    def kernel(keep_ref, other_ref, *outs):
        for l in range(layers):
            for b in range(NY):
                rows = slice(b * OWN, (b + 1) * OWN)
                total = keep_ref[l, rows].astype(F32) + other_ref[l, rows].astype(F32)
                outs[b][l] = total.astype(outs[b].dtype)

    outs = [shape((layers, OWN, feats), F32 if b == 0 else wire) for b in range(NY)]
    return call(kernel, outs, [keep, other], "half_sum")


def activate(parts, bias, active):
    layers, own, feats = parts[0].shape
    blocks = active.shape[2]
    wide = feats // blocks

    def kernel(*refs):
        *part_refs, bias_ref, active_ref, out_ref = refs
        block = lax.axis_index("core") * 2 + lax.axis_index("y") // 2
        for l in range(layers):
            pre = part_refs[0][l]
            for ref in part_refs[1:]:
                pre = pre + ref[l]
            pre = jnp.maximum(pre + bias_ref[l : l + 1, :].astype(F32), 0.0)
            for j in range(blocks):
                on = active_ref[l, block, j].astype(F32)
                out_ref[l, :, j * wide : (j + 1) * wide] = (pre[:, j * wide : (j + 1) * wide] * on).astype(BF16)

    ins = [*parts, bias, active]
    return call(
        kernel, [shape((layers, own, feats), BF16)], ins, "activate", in_specs=[VMEM] * (len(ins) - 1) + [SMEM]
    )[0]


def decode(parts, dec_weight):
    layers, own, feats = parts[0].shape
    width = dec_weight.shape[2]
    tokens = own * len(parts)

    def kernel(*refs):
        part_refs, refs = refs[: len(parts)], refs[len(parts) :]
        w_ref, out_refs, (feat_ref, weights) = refs[0], refs[1 : 1 + 2 * NX], refs[1 + 2 * NX :]

        @pl.when(pl.program_id(0) == 0)
        def _():
            for l in range(layers):
                for k, ref in enumerate(part_refs):
                    feat_ref[pl.ds(k * own, own), l * feats : (l + 1) * feats] = ref[l]

        for t in range(layers):
            depth = (t + 1) * feats

            @pl.when(pl.program_id(0) == t)
            def _():
                for s in range(t + 1):
                    weights[pl.ds(s * feats, feats), :] = w_ref[pair(s, t)]
                total = jnp.dot(feat_ref[:, :depth], weights[:depth, :], preferred_element_type=F32).astype(BF16)
                for s in range(NZ):
                    for q in range(NX):
                        at = (s * NX + q) * ROWS
                        out_refs[t // HALF * NX + q][t % HALF, s] = total[at : at + ROWS]

    outs = [shape((HALF, NZ, ROWS, width), BF16)] * (2 * NX) + [shape((tokens, layers * feats), BF16)]
    flops = layers * (layers + 1) * tokens * feats * width
    *terms, features = call(
        kernel, outs, [*parts, dec_weight], "decode", (layers,), None, None,
        [pltpu.VMEM((layers * feats, width), BF16)], flops, 24,
    )
    return terms[:NX], terms[NX:], features


def relay(ours, passing):
    block = (1,) + ours[0].shape[1:]

    def kernel(*refs):
        for k in range(2):
            refs[4 + k][...] = (refs[k][...].astype(F32) + refs[2 + k][...].astype(F32)).astype(BF16)

    spec = pl.BlockSpec(block, lambda l: (l, 0, 0, 0))
    return call(
        kernel, [shape(ours[0].shape, BF16)] * 2, [*ours, *passing], "relay", (ours[0].shape[0],), [spec] * 4, [spec] * 2
    )


def line_sum(low, high):
    targets, _, rows, width = low[0].shape
    count = len(low)

    def kernel(*refs):
        z = lax.axis_index("z")
        out_refs = refs[2 * count :]
        for h in range(2):
            part_refs = refs[h * count : (h + 1) * count]
            for j in range(NZ):
                s = lax.rem(z + j, NZ)
                for l in range(targets):
                    total = part_refs[0][l, s].astype(F32)
                    for ref in part_refs[1:]:
                        total = total + ref[l, s].astype(F32)
                    out_refs[j][h * targets + l] = total.astype(BF16)

    return call(kernel, [shape((2 * targets, rows, width), BF16)] * NZ, [*low, *high], "line_sum")


def residual_rows(parts, own_targets):
    layers, rows, width = parts[0].shape

    def kernel(*refs):
        part_refs, target_ref, out_ref = refs[:NZ], refs[NZ], refs[NZ + 1]
        for l in range(layers):
            total = part_refs[0][l].astype(F32)
            for ref in part_refs[1:]:
                total = total + ref[l].astype(F32)
            out_ref[l] = (total - target_ref[l].astype(F32)).astype(BF16)

    return call(kernel, [shape((layers, rows, width), BF16)], [*parts, own_targets], "residual")[0]


def line_up(parts, order):
    layers, rows, width = parts[0].shape

    def kernel(*refs):
        part_refs, out_refs = refs[:NZ], refs[NZ:]
        z = lax.axis_index("z")
        for ref, j in zip(part_refs, order):
            s = lax.rem(z + j, NZ)
            for l in range(layers):
                out_refs[l // HALF][l % HALF, s] = ref[l]

    return call(kernel, [shape((HALF, NZ, rows, width), BF16)] * 2, parts, "line_up")


def assemble(refs, out):
    for l in range(out.shape[0]):
        for s in range(NZ):
            for q in range(NX):
                out[l, pl.ds((s * NX + q) * ROWS, ROWS), :] = refs[l // HALF * NX + q][l % HALF, s]


def backward(planes, dec_weight):
    feats, width = dec_weight.shape[1:]
    tokens = NZ * NX * ROWS
    half = tokens // NC

    def kernel(*refs):
        plane_refs, refs = refs[: len(planes)], refs[len(planes) :]
        w_ref, keep_ref, send_ref, resid, weights = refs

        @pl.when(pl.program_id(0) == 0)
        def _():
            for m in range(LAYERS):
                for s in range(NZ):
                    for q in range(NX):
                        at = pl.ds((s * NX + q) * ROWS, ROWS)
                        resid[at, m * width : (m + 1) * width] = plane_refs[m // HALF * NX + q][m % HALF, s]

        for l in range(LAYERS):

            @pl.when(pl.program_id(0) == l)
            def _():
                for m in range(l, LAYERS):
                    weights[:, m * width : (m + 1) * width] = w_ref[pair(l, m)]
                total = lax.dot_general(
                    resid[:, l * width :], weights[:, l * width :], (((1,), (1,)), ((), ())), preferred_element_type=F32
                )
                keep_ref[l] = total[:half]
                send_ref[l] = total[half:].astype(BF16)

    flops = LAYERS * (LAYERS + 1) * tokens * feats * width
    return call(
        kernel, [shape((LAYERS, half, feats), F32), shape((LAYERS, half, feats), BF16)],
        [*planes, dec_weight], "backward", (LAYERS,), None, None,
        [pltpu.VMEM((tokens, LAYERS * width), BF16), pltpu.VMEM((feats, LAYERS * width), BF16)], flops, 28,
    )


def decoder_grads(features, planes):
    layers, tokens = LAYERS, features.shape[0]
    feats, width = features.shape[1] // layers, planes[0].shape[3]
    pairs = layers * (layers + 1) // 2

    def source_target(i):
        s = (i >= 4) * 1 + (i >= 7) * 1 + (i >= 9) * 1
        return s, i - (s * LAYERS - s * (s - 1) // 2) + s

    def kernel(*refs):
        plane_refs, (feat_ref, out_ref, resid) = refs[: len(planes)], refs[len(planes) :]
        i = pl.program_id(0)
        source, target = source_target(i)

        @pl.when(i == 0)
        def _():
            assemble(plane_refs, resid)

        out_ref[0] = lax.dot_general(
            feat_ref[:, pl.ds(pl.multiple_of(source * feats, feats), feats)], resid[target],
            (((0,), (0,)), ((), ())), preferred_element_type=F32,
        ).astype(BF16)

    return call(
        kernel, [shape((pairs, feats, width), BF16)], [*planes, features], "decoder_grads", (pairs,),
        [VMEM] * (len(planes) + 1), [pl.BlockSpec((1, feats, width), lambda i: (i, 0, 0))],
        [pltpu.VMEM((layers, tokens, width), BF16)], 2 * pairs * tokens * feats * width, 24,
    )[0]


def mask_grad(parts, own_feats):
    layers, own, feats = own_feats.shape

    def kernel(*refs):
        part_refs, feat_ref, out_ref = refs[:NY], refs[NY], refs[NY + 1]
        for l in range(layers):
            total = part_refs[0][l].astype(F32)
            for ref in part_refs[1:]:
                total = total + ref[l].astype(F32)
            out_ref[l] = jnp.where(feat_ref[l].astype(F32) > 0, total, 0.0).astype(BF16)

    return call(kernel, [shape((layers, own, feats), BF16)], [*parts, own_feats], "mask_grad")[0]


def encoder_grads(parts, inputs):
    layers, tokens, width = inputs.shape
    own, feats = parts[0].shape[1:]

    def kernel(*refs):
        part_refs, (in_ref, grad_ref, bias_ref, whole) = refs[: len(parts)], refs[len(parts) :]
        total = jnp.zeros((1, feats), F32)
        places = spots()
        for k, ref in enumerate(part_refs):
            for q in range(NX):
                whole[pl.ds(places[k * NX + q], ROWS), :] = ref[0, q * ROWS : (q + 1) * ROWS, :]
            total = total + jnp.sum(ref[0].astype(F32), axis=0, keepdims=True)
        bias_ref[pl.ds(pl.program_id(0), 1), :] = total
        grad_ref[0] = lax.dot_general(
            in_ref[0], whole[...], (((0,), (0,)), ((), ())), preferred_element_type=F32
        ).astype(BF16)

    grad, bias = call(
        kernel, [shape((layers, width, feats), BF16), shape((layers, feats), F32)], [*parts, inputs],
        "encoder_grads", (layers,), [per_layer(own, feats)] * len(parts) + [per_layer(tokens, width)],
        [per_layer(width, feats), VMEM], [pltpu.VMEM((tokens, feats), BF16)],
        2 * layers * tokens * width * feats, 16,
    )
    return grad, bias


def gather_col(own):
    mine = [own] + [shift(own, "y", NY, -k) for k in range(1, NY)]
    return mine + [shift(part, "core", NC, 1) for part in mine]


def scatter_col(pieces):
    return [pieces[0]] + [shift(pieces[k], "y", NY, k) for k in range(1, NY)]


def scatter_x(low, high):
    passing = [shift(low[2], "x", NX, 1), shift(high[2], "x", NX, -1)]
    high_1, low_3 = shift(high[1], "x", NX, 1), shift(low[3], "x", NX, -1)
    low_1, high_3 = relay([low[1], high[3]], passing)
    low_1, high_3 = shift(low_1, "x", NX, 1), shift(high_3, "x", NX, -1)
    return [low[0], low_1, low_3], [high[0], high_1, high_3]


def gather_x(low, high):
    low_3, high_1 = shift(low, "x", NX, 1), shift(high, "x", NX, -1)
    high_3, low_1 = shift(high, "x", NX, 1), shift(low, "x", NX, -1)
    low_2, high_2 = shift(low_3, "x", NX, 1), shift(high_1, "x", NX, -1)
    return [low, low_1, low_2, low_3, high, high_1, high_2, high_3]


def body(inputs, targets, enc_weight, enc_bias, dec_weight, active_blocks):
    keep, send = encode(inputs, enc_weight)
    keep, targets = lax.optimization_barrier((keep, targets))
    own_targets = lax.ppermute(targets, ("x", "z", "y", "core"), target_moves()).transpose(1, 0, 2)
    pieces = split_half(keep, shift(send, "core", NC, 1), F32)
    own_feats = activate(scatter_col(pieces), enc_bias, active_blocks)
    low, high, features = decode(gather_col(own_feats), dec_weight)
    pieces = line_sum(*scatter_x(low, high))
    mine = residual_rows([pieces[0]] + [shift(pieces[k], "z", NZ, k) for k in Z_ORDER], own_targets)
    low, high = line_up([mine] + [shift(mine, "z", NZ, -k) for k in Z_ORDER], (0,) + Z_ORDER)
    planes = gather_x(low, high)
    keep, send = backward(planes, dec_weight)
    pieces = split_half(keep, shift(send, "core", NC, 1), BF16)
    pieces, features = lax.optimization_barrier((pieces, features))
    dec_grad = decoder_grads(features, planes)
    parts = scatter_col(pieces)
    parts, dec_grad = lax.optimization_barrier((parts, dec_grad))
    own_grad = mask_grad(parts, own_feats)
    enc_grad, bias_grad = encoder_grads(gather_col(own_grad), inputs)
    return enc_grad, bias_grad, dec_grad


def solution(mesh):
    grid = Mesh(mesh.devices.reshape(NX, NZ, NY, NC), ("x", "z", "y", "core"))
    lay, col = ("x", "z"), ("y", "core")
    return jax.shard_map(
        body,
        mesh=grid,
        in_specs=(P(None, None, col), P(lay, None, col), P(None, col, lay), P(None, lay), P(None, lay, col), P(None, None, lay)),
        out_specs=(P(None, col, lay), P(None, lay), P(None, lay, col)),
        check_vma=False,
    )
```
